32 devices in a mesh: layer: 8 (over y, x, core), wave: 4 (over z).
Axes of the slice: x: 2, y: 2, z: 4, core: 2. Of those that a mesh axis runs over, the one named last changes fastest.
Arguments:
- eps_harmonics: float32 [8, 2, 255], P('layer'), may hold values from -4 to 4
- eigen_modes: float32 [8, 4, 2, 128, 128], P('layer', 'wave'), may hold values from -1 to 2
- mode_phase: float32 [8, 4, 128], P('layer', 'wave'), may hold values from -3.140625 to 3.140625
- mode_decay: float32 [8, 4, 128], P('layer', 'wave'), may hold values from 0.002 to 0.1
- retained_orders: int32 [4], P('wave'), may hold values from 64 to 128, as said below
- reflect_cotangent: float32 [4, 2, 128, 128], P('wave'), may hold values from -6 to 6
Outputs:
- eps_gradient: float32 [8, 2, 255], P('layer')
- mode_gradient: float32 [8, 4, 2, 128, 128], P('layer', 'wave')
The draws below stay inside these ranges and needn't reach their ends.
Inputs may be any that keep to these rules, and one draw needn't show every extreme that they name: `retained_orders`: in every draw some wavelength retains all 128 orders and another retains 128 // 2.
All inputs are finite; a program needn't handle non-finite values.
Results may differ from the reference program's by a relative error of at most 0.0003.
Values sent between devices are 32-bit elements; how exact they have to be, the bound alone decides.
A program may use at most 64 MiB of HBM per device.

```python
import math
import jax
import jax.numpy as jnp
from jax import lax

ORDERS = 128
HARM = 255
WAVES = 4
LAYERS = 8


def draw_eps_harmonics(key, part):
    shape_full = (LAYERS, 2, HARM)
    harm_key = jax.random.fold_in(key, 21)
    values = jnp.clip(2.4 * jax.random.normal(harm_key, shape_full, jnp.float32), -4.0, 4.0)
    return values


def draw_eigen_modes(key, part):
    spread_scale = 0.3 / math.sqrt(ORDERS)
    shape_full = (LAYERS, WAVES, 2, ORDERS, ORDERS)
    mixing = jnp.clip(jax.random.normal(key, shape_full, jnp.float32), -4.0, 4.0)
    unit_matrix = jnp.eye(ORDERS, dtype=jnp.float32)
    real_identity = jnp.stack([unit_matrix, jnp.zeros_like(unit_matrix)])
    return real_identity + spread_scale * mixing


def draw_retained_orders(key, part):
    counts_drawn = jax.random.randint(jax.random.fold_in(key, 11), (WAVES,), ORDERS // 2, ORDERS + 1, dtype=jnp.int32)
    first_pick = jax.random.randint(jax.random.fold_in(key, 12), (), 0, WAVES, dtype=jnp.int32)
    second_pick = (first_pick + 1) % WAVES
    counts_drawn = counts_drawn.at[first_pick].set(ORDERS)
    counts_drawn = counts_drawn.at[second_pick].set(ORDERS // 2)
    return counts_drawn.astype(jnp.int32)


def block_scale(rng, shape, cuts, least, top_value):
    def one(dim, shards_of):
        draws = jax.random.uniform(jax.random.fold_in(jax.random.fold_in(rng, 6), dim), (shards_of,), jnp.float32, least / len(cuts), top_value / len(cuts))
        return jnp.repeat(jnp.exp(draws), shape[dim] // shards_of).reshape((-1,) + (1,) * (len(shape) - dim - 1))

    level = one(*cuts[0])
    for cut in cuts[1:]:
        level = level * one(*cut)
    return level


def bell_draw(key, extent, deviation, most, split=(), kind=jnp.bfloat16):
    values = jax.random.normal(key, extent, jnp.float32) * deviation
    if len(split) > 0:
        values = block_scale(key, extent, split, -0.22, 0.18) * values
    return jnp.clip(values, min=-most, max=most).astype(kind)


def setup_inputs(seed: int = 0) -> dict:
    streams_of = jax.random.split(jax.random.key(seed), 7)
    return {
        "eps_harmonics": draw_eps_harmonics(jax.random.fold_in(streams_of[6], 71), 0),
        "eigen_modes": draw_eigen_modes(jax.random.fold_in(streams_of[6], 71), 0),
        "mode_phase": jnp.clip(jax.random.uniform(streams_of[2], (LAYERS, WAVES, ORDERS), jnp.float32, -3.140625, 3.140625), -3.140625, 3.140625),
        "mode_decay": jnp.clip(jnp.exp(math.log(0.1) - 3.912023 * jax.random.uniform(streams_of[3], (LAYERS, WAVES, ORDERS), jnp.float32) ** block_scale(streams_of[3], (LAYERS, WAVES, ORDERS), ((0, 8), (1, 4)), -0.2, 0.2)), 0.002, 0.1),
        "retained_orders": draw_retained_orders(jax.random.fold_in(streams_of[6], 71), 0),
        "reflect_cotangent": bell_draw(streams_of[5], (WAVES, 2, ORDERS, ORDERS), 1.0, 6.0, ((0, 4),), jnp.float32),
    }


SHEET_TRANSMISSION = 0.9
INVERSE_STEPS = 4

def complex_product(left_side, right_side):
    highest = lax.Precision.HIGHEST
    real_part = jnp.dot(left_side[0], right_side[0], precision=highest, preferred_element_type=jnp.float32) - jnp.dot(left_side[1], right_side[1], precision=highest, preferred_element_type=jnp.float32)
    imag_part = jnp.dot(left_side[0], right_side[1], precision=highest, preferred_element_type=jnp.float32) + jnp.dot(left_side[1], right_side[0], precision=highest, preferred_element_type=jnp.float32)
    return jnp.stack([real_part, imag_part])

def complex_identity(order_count):
    unit_matrix = jnp.eye(order_count, dtype=jnp.float32)
    return jnp.stack([unit_matrix, jnp.zeros((order_count, order_count), jnp.float32)])

def complex_solve(system, right_side):
    identity = complex_identity(system.shape[-1])
    inverse = 2.0 * identity - system
    for step_index in range(INVERSE_STEPS):
        inverse = complex_product(inverse, 2.0 * identity - complex_product(system, inverse))
    return complex_product(inverse, right_side)

def star_product(upper_stack, lower_stack):
    identity = complex_identity(upper_stack[0].shape[-1])
    down_wave = complex_solve(identity - complex_product(upper_stack[3], lower_stack[0]), upper_stack[2])
    up_wave = complex_solve(identity - complex_product(lower_stack[0], upper_stack[3]), lower_stack[1])
    return (upper_stack[0] + complex_product(upper_stack[1], complex_product(lower_stack[0], down_wave)), complex_product(upper_stack[1], up_wave), complex_product(lower_stack[2], down_wave), lower_stack[3] + complex_product(lower_stack[2], complex_product(upper_stack[3], up_wave)))

def order_window(kept_count, order_count):
    order_numbers = jnp.arange(order_count, dtype=jnp.int32) - order_count // 2
    half_count = kept_count // 2
    return ((order_numbers >= -half_count) & (order_numbers < kept_count - half_count)).astype(jnp.float32)

def toeplitz(harmonics, order_count):
    offsets = jnp.arange(order_count, dtype=jnp.int32)[:, None] - jnp.arange(order_count, dtype=jnp.int32)[None, :] + (order_count - 1)
    return harmonics[:, offsets]

def layer_blocks(toeplitz_matrix, mode_matrix, phases, attenuation, window):
    order_count = mode_matrix.shape[-1]
    sheet_scale = 1.0 / (5.0 * math.sqrt(2 * order_count - 1))
    coupled = complex_product(toeplitz_matrix, mode_matrix) * sheet_scale
    sheet_matrix = coupled * window[None, :, None] * window[None, None, :]
    magnitude = window * jnp.exp(-attenuation)
    prop_real = magnitude * jnp.cos(phases)
    prop_imag = magnitude * jnp.sin(phases)
    outer_real = prop_real[:, None] * prop_real[None, :] - prop_imag[:, None] * prop_imag[None, :]
    outer_imag = prop_real[:, None] * prop_imag[None, :] + prop_imag[:, None] * prop_real[None, :]
    back_reflection = jnp.stack([outer_real * sheet_matrix[0] - outer_imag * sheet_matrix[1], outer_real * sheet_matrix[1] + outer_imag * sheet_matrix[0]])
    unit_matrix = jnp.eye(order_count, dtype=jnp.float32)
    through = SHEET_TRANSMISSION * jnp.stack([unit_matrix * prop_real[None, :], unit_matrix * prop_imag[None, :]])
    return (sheet_matrix, through, through, back_reflection)

def reference(eps_harmonics, eigen_modes, mode_phase, mode_decay, retained_orders, reflect_cotangent):
    order_total = eigen_modes.shape[-1]

    def one_wavelength(inputs):
        modes_here, phase_here, decay_here, kept_count, cotangent_here = inputs
        window = order_window(kept_count, order_total)

        def total_reflection(harmonics_all, modes_all):
            stacked = None
            for position in range(LAYERS):
                blocks = layer_blocks(toeplitz(harmonics_all[position], order_total), modes_all[position], phase_here[position], decay_here[position], window)
                stacked = blocks if stacked is None else star_product(stacked, blocks)
            return stacked[0]
        _, pullback = jax.vjp(total_reflection, eps_harmonics, modes_here)
        return pullback(cotangent_here)
    per_wave = (jnp.moveaxis(eigen_modes, 1, 0), jnp.moveaxis(mode_phase, 1, 0), jnp.moveaxis(mode_decay, 1, 0), retained_orders, reflect_cotangent)
    eps_parts, mode_parts = lax.map(one_wavelength, per_wave)
    return (lax.optimization_barrier(jnp.sum(eps_parts, axis=0)), jnp.moveaxis(mode_parts, 0, 1))
```

```python
import functools
import math

import jax
import jax.numpy as jnp
from jax import lax
from jax.experimental import pallas as pl
from jax.experimental.pallas import tpu as pltpu
from jax.sharding import PartitionSpec as P

TRANSMISSION = 0.9
LEVELS = 5
F32 = jnp.float32
BF16 = jnp.bfloat16


def split(x):
    hi = x.astype(BF16)
    return hi, (x - hi.astype(F32)).astype(BF16)


def embed(b):
    n = b.shape[0]
    return jnp.concatenate([b, jnp.concatenate([-b[:, n:], b[:, :n]], axis=1)], axis=0)


def weights(parts):
    return embed(parts[0]), embed(parts[1])


def real_dot(a, b):
    return jnp.dot(a, b, preferred_element_type=F32)


def products(lefts, weight):
    n = lefts[0][0].shape[0]
    high, low = weight
    first = real_dot(jnp.concatenate([part for left in lefts for part in left], axis=0), high)
    second = real_dot(jnp.concatenate([left[0] for left in lefts], axis=0), low)
    return [
        first[2 * i * n : (2 * i + 1) * n]
        + first[(2 * i + 1) * n : (2 * i + 2) * n]
        + second[i * n : (i + 1) * n]
        for i in range(len(lefts))
    ]


def product(left, right):
    return products([left], weights(right))[0]


def scaled(a, b):
    n = a.shape[0]
    ar, ai, br, bi = a[:, :n], a[:, n:], b[:, :n], b[:, n:]
    return jnp.concatenate([ar * br - ai * bi, ar * bi + ai * br], axis=1)


def conj_transpose(a):
    n = a.shape[0]
    return jnp.concatenate([a[:, :n].T, -a[:, n:].T], axis=1)


def spread_rows(prop):
    n = prop.shape[-1] // 2
    return jnp.broadcast_to(prop, (n, 2 * n))


def spread_columns(prop):
    n = prop.shape[-1] // 2
    rows = spread_rows(prop)
    return jnp.concatenate([rows[:, :n].T, rows[:, n:].T], axis=1)


def outer(prop):
    return scaled(spread_columns(prop), spread_rows(prop))


def series(start, base):
    starts, powers = [], []
    value, power = start, base
    for level in range(LEVELS):
        value_parts, power_parts = split(value), split(power)
        starts.append(value_parts)
        powers.append(power_parts)
        weight = weights(power_parts)
        if level + 1 < LEVELS:
            step, power = products([value_parts, power_parts], weight)
        else:
            (step,) = products([value_parts], weight)
        value = value + step
    return value, starts, powers


def series_back(starts, powers, cotangent, need_start):
    power_bar = None
    for level in reversed(range(LEVELS)):
        parts = split(cotangent)
        total = product(parts, starts[level])
        if power_bar is not None:
            bar_parts = split(power_bar)
            total = total + product(bar_parts, powers[level])
            total = total + product(powers[level], bar_parts)
        if level > 0 or need_start:
            cotangent = cotangent + product(powers[level], parts)
        power_bar = total
    return power_bar, cotangent


def order_mask(count, n):
    half = count // 2
    row = lax.broadcasted_iota(jnp.int32, (n, n), 0) - n // 2
    column = lax.broadcasted_iota(jnp.int32, (n, n), 1) - n // 2
    keep = (row >= -half) & (row < count - half) & (column >= -half) & (column < count - half)
    return keep.astype(F32)


def toeplitz_of(harm_ref, n):
    def one(part):
        rows = jnp.broadcast_to(harm_ref[part : part + 1, :], (n, 2 * n))
        rolled = pltpu.roll(rows, n + 1, 1, stride=1, stride_axis=0)
        return rolled[:, :n].T

    return jnp.concatenate([one(0), one(1)], axis=1)


def sheet_kernel(count_ref, harm_ref, mode_ref, phase_ref, decay_ref, pack_ref):
    n = mode_ref.shape[-1]
    count = count_ref[0]
    toeplitz = toeplitz_of(harm_ref, n)
    modes = jnp.concatenate([mode_ref[0], mode_ref[1]], axis=1)
    mask = order_mask(count, n) * (1.0 / (5.0 * math.sqrt(2 * n - 1)))
    coupled = product(split(toeplitz), split(modes))
    pack_ref[:n, :] = coupled * jnp.concatenate([mask, mask], axis=1)
    order = lax.broadcasted_iota(jnp.int32, (1, n), 1) - n // 2
    window = ((order >= -(count // 2)) & (order < count - count // 2)).astype(F32)
    magnitude = window * jnp.exp(-decay_ref[...])
    phase = phase_ref[...]
    prop = jnp.concatenate([magnitude * jnp.cos(phase), magnitude * jnp.sin(phase)], axis=1)
    pack_ref[n:, :] = jnp.broadcast_to(prop, (8, 2 * n))


def chain_kernel(
    layers, count_ref, harm_ref, mode_ref, cot_ref, pack_ref, eps_ref, grad_ref,
    below, back, left, right, bar,
):
    n = mode_ref.shape[-1]
    through = TRANSMISSION
    both = through * through
    me = lax.axis_index("layer")

    def sheet(i):
        return pack_ref[i, :n, :]

    def prop(i):
        return pack_ref[i, n : n + 1, :]

    below[...] = scaled(outer(prop(layers - 2)), sheet(layers - 1))

    def go_up(step, carry):
        i = layers - 2 - step
        here = sheet(i)
        start = below[...]
        base = product(split(here), split(start))
        value, _, _ = series(start, base)
        below[...] = scaled(outer(prop(i - 1)), here + both * value)
        return carry

    lax.fori_loop(0, jnp.maximum(layers - 2 - me, 0), go_up, 0)

    @pl.when(me == layers - 1)
    def _():
        below[...] = jnp.zeros_like(below)

    unit = (
        lax.broadcasted_iota(jnp.int32, (n, n), 0) == lax.broadcasted_iota(jnp.int32, (n, n), 1)
    ).astype(F32)
    unit = jnp.concatenate([unit, unit], axis=1)
    back[...] = scaled(outer(prop(0)), sheet(0))
    left[...] = through * unit * prop(0)
    right[...] = through * unit * prop(0)

    def go_down(i, carry):
        here = split(sheet(i))
        value, into, out = back[...], left[...], right[...]
        value_parts = split(value)
        power = product(here, value_parts)
        other = product(value_parts, here)
        for level in range(LEVELS):
            power_parts, other_parts = split(power), split(other)
            weight = weights(power_parts)
            last = level + 1 == LEVELS
            lefts = [split(value), split(into)] + ([] if last else [power_parts])
            steps = products(lefts, weight)
            value, into = value + steps[0], into + steps[1]
            out = out + product(other_parts, split(out))
            if not last:
                power = steps[2]
                other = product(other_parts, other_parts)
        p = prop(i)
        back[...] = scaled(outer(p), sheet(i) + both * value)
        left[...] = through * scaled(into, spread_rows(p))
        right[...] = through * scaled(spread_columns(p), out)
        return carry

    lax.fori_loop(1, jnp.maximum(me, 1), go_down, 0)

    here = sheet(me)
    start = below[...]
    base = product(split(here), split(start))
    value, starts, powers = series(start, base)
    reflection = here + both * value
    bar[...] = conj_transpose(jnp.concatenate([cot_ref[0], cot_ref[1]], axis=1))

    @pl.when(me > 0)
    def _():
        above = split(back[...])
        above_base = product(above, split(reflection))
        _, above_starts, above_powers = series(reflection, above_base)
        inner = product(split(product(split(right[...]), split(bar[...]))), split(left[...]))
        base_bar, start_bar = series_back(above_starts, above_powers, inner, True)
        bar[...] = start_bar + product(split(base_bar), above)

    sheet_bar = bar[...]
    base_bar, _ = series_back(starts, powers, both * sheet_bar, False)
    sheet_bar = sheet_bar + product(split(start), split(base_bar))
    mask = order_mask(count_ref[0], n) * (1.0 / (5.0 * math.sqrt(2 * n - 1)))
    coupled_bar = split(sheet_bar * jnp.concatenate([mask, mask], axis=1))
    modes = jnp.concatenate([mode_ref[0], mode_ref[1]], axis=1)
    mode_bar = conj_transpose(product(coupled_bar, split(toeplitz_of(harm_ref, n))))
    grad_ref[0] = mode_bar[:, :n]
    grad_ref[1] = mode_bar[:, n:]
    flip = (
        lax.broadcasted_iota(jnp.int32, (n, n), 0) + lax.broadcasted_iota(jnp.int32, (n, n), 1)
        == n - 1
    ).astype(F32).astype(BF16)
    flipped = tuple(real_dot(flip, part).astype(BF16) for part in split(modes))
    toeplitz_bar = product(flipped, coupled_bar)
    zeros = jnp.zeros((n, n), F32)

    def fold(part):
        wide = jnp.concatenate([part, zeros], axis=1)
        rolled = pltpu.roll(wide, 0, 1, stride=1, stride_axis=0)
        return jnp.sum(rolled, axis=0, keepdims=True)

    eps_ref[0:1, :] = fold(toeplitz_bar[:, :n])
    eps_ref[1:2, :] = -fold(toeplitz_bar[:, n:])


def per_device(
    layers, eps_harmonics, eigen_modes, mode_phase, mode_decay, retained_orders, reflect_cotangent
):
    n = eigen_modes.shape[-1]
    vmem = pl.BlockSpec(memory_space=pltpu.VMEM)
    smem = pl.BlockSpec(memory_space=pltpu.SMEM)
    params = pltpu.CompilerParams(vmem_limit_bytes=48 * 1024 * 1024)
    harmonics = jnp.pad(eps_harmonics[0], ((0, 0), (0, 1)))
    modes = eigen_modes[0, 0]
    pack = pl.pallas_call(
        sheet_kernel,
        out_shape=jax.ShapeDtypeStruct((n + 8, 2 * n), F32),
        in_specs=[smem] + [vmem] * 4,
        out_specs=vmem,
        compiler_params=params,
        name="sheet",
    )(retained_orders, harmonics, modes, mode_phase[0], mode_decay[0])
    packs = lax.all_gather(pack, "layer")
    eps_part, grad = pl.pallas_call(
        functools.partial(chain_kernel, layers),
        out_shape=(
            jax.ShapeDtypeStruct((2, 2 * n), F32),
            jax.ShapeDtypeStruct((2, n, n), F32),
        ),
        in_specs=[smem] + [vmem] * 4,
        out_specs=(vmem, vmem),
        scratch_shapes=[pltpu.VMEM((n, 2 * n), F32) for _ in range(5)],
        compiler_params=params,
        name="chain",
    )(retained_orders, harmonics, modes, reflect_cotangent[0], packs)
    eps_grad = lax.psum(eps_part, "wave")[:, : 2 * n - 1]
    return eps_grad[None], grad[None, None]


def solution(mesh):
    placed = (
        P("layer", None, None),
        P("layer", "wave", None, None, None),
        P("layer", "wave", None),
        P("layer", "wave", None),
        P("wave"),
        P("wave", None, None, None),
    )
    return jax.shard_map(
        functools.partial(per_device, mesh.shape["layer"]),
        mesh=mesh,
        in_specs=placed,
        out_specs=(P("layer", None, None), P("layer", "wave", None, None, None)),
        check_vma=False,
    )
```

```python
import functools
import math

import jax
import jax.numpy as jnp
from jax import lax
from jax.experimental import pallas as pl
from jax.experimental.pallas import tpu as pltpu
from jax.sharding import PartitionSpec as P

TRANSMISSION = 0.9
LEVELS = 5
F32 = jnp.float32
BF16 = jnp.bfloat16
MESH = pl.DeviceIdType.MESH


def split(x):
    hi = x.astype(BF16)
    return hi, (x - hi.astype(F32)).astype(BF16)


def embed(b):
    n = b.shape[0]
    return jnp.concatenate([b, jnp.concatenate([-b[:, n:], b[:, :n]], axis=1)], axis=0)


def weights(parts):
    return embed(parts[0]), embed(parts[1])


def real_dot(a, b):
    return jnp.dot(a, b, preferred_element_type=F32)


def products(lefts, weight):
    n = lefts[0][0].shape[0]
    high, low = weight
    first = real_dot(jnp.concatenate([part for left in lefts for part in left], axis=0), high)
    second = real_dot(jnp.concatenate([left[0] for left in lefts], axis=0), low)
    return [
        first[2 * i * n : (2 * i + 1) * n]
        + first[(2 * i + 1) * n : (2 * i + 2) * n]
        + second[i * n : (i + 1) * n]
        for i in range(len(lefts))
    ]


def product(left, right):
    return products([left], weights(right))[0]


def scaled(a, b):
    n = a.shape[0]
    ar, ai, br, bi = a[:, :n], a[:, n:], b[:, :n], b[:, n:]
    return jnp.concatenate([ar * br - ai * bi, ar * bi + ai * br], axis=1)


def conj_transpose(a):
    n = a.shape[0]
    return jnp.concatenate([a[:, :n].T, -a[:, n:].T], axis=1)


def spread_rows(prop):
    n = prop.shape[-1] // 2
    return jnp.broadcast_to(prop, (n, 2 * n))


def spread_columns(prop):
    n = prop.shape[-1] // 2
    rows = spread_rows(prop)
    return jnp.concatenate([rows[:, :n].T, rows[:, n:].T], axis=1)


def outer(prop):
    return scaled(spread_columns(prop), spread_rows(prop))


def series(start, base):
    starts, powers = [], []
    value, power = start, base
    for level in range(LEVELS):
        value_parts, power_parts = split(value), split(power)
        starts.append(value_parts)
        powers.append(power_parts)
        weight = weights(power_parts)
        if level + 1 < LEVELS:
            step, power = products([value_parts, power_parts], weight)
        else:
            (step,) = products([value_parts], weight)
        value = value + step
    return value, starts, powers


def series_back(starts, powers, cotangent, need_start):
    power_bar = None
    for level in reversed(range(LEVELS)):
        parts = split(cotangent)
        total = product(parts, starts[level])
        if power_bar is not None:
            bar_parts = split(power_bar)
            total = total + product(bar_parts, powers[level])
            total = total + product(powers[level], bar_parts)
        if level > 0 or need_start:
            cotangent = cotangent + product(powers[level], parts)
        power_bar = total
    return power_bar, cotangent


def order_mask(count, n):
    half = count // 2
    row = lax.broadcasted_iota(jnp.int32, (n, n), 0) - n // 2
    column = lax.broadcasted_iota(jnp.int32, (n, n), 1) - n // 2
    keep = (row >= -half) & (row < count - half) & (column >= -half) & (column < count - half)
    return keep.astype(F32)


def toeplitz_of(harm_ref, n):
    def one(part):
        harmonics = jnp.concatenate([harm_ref[part : part + 1, :], jnp.zeros((1, 1), F32)], axis=1)
        rows = jnp.broadcast_to(harmonics, (n, 2 * n))
        rolled = pltpu.roll(rows, n + 1, 1, stride=1, stride_axis=0)
        return rolled[:, :n].T

    return jnp.concatenate([one(0), one(1)], axis=1)


def kernel(
    layers, waves, count_ref, harm_in, mode_in, phase_in, decay_in, cot_in, eps_ref, grad_ref,
    pack_ref, harm_ref, mode_ref, phase_ref, decay_ref, cot_ref, below, back, left, right, bar,
    eps_slots, in_sem, send_sem, recv_sem, pass_sem, eps_send, eps_recv,
):
    n = mode_ref.shape[-1]
    through = TRANSMISSION
    both = through * through
    me = lax.axis_index("layer")
    wave = lax.axis_index("wave")
    other_core = me + 1 - 2 * lax.rem(me, 2)
    far = range(1, layers // 2)

    def ahead(hop):
        return lax.rem(me + 2 * hop, layers)

    def behind(hop):
        return lax.rem(me + layers - 2 * hop, layers)

    def wave_ahead(hop):
        return lax.rem(wave + hop, waves)

    loads = [
        pltpu.make_async_copy(source, target, in_sem.at[i])
        for i, (source, target) in enumerate(
            (
                (harm_in.at[0], harm_ref),
                (mode_in.at[0, 0], mode_ref),
                (phase_in.at[0], phase_ref),
                (decay_in.at[0], decay_ref),
                (cot_in.at[0], cot_ref),
            )
        )
    ]
    for load in loads:
        load.start()
    barrier = pltpu.get_barrier_semaphore()
    peers = [{"layer": other_core}] + [{"layer": ahead(hop)} for hop in far]
    peers = peers + [{"wave": wave_ahead(hop)} for hop in range(1, waves)]
    for peer in peers:
        pl.semaphore_signal(barrier, inc=1, device_id=peer, device_id_type=MESH)
    for load in loads:
        load.wait()

    count = count_ref[0]
    modes = split(jnp.concatenate([mode_ref[0], mode_ref[1]], axis=1))
    toeplitz = split(toeplitz_of(harm_ref, n))
    mask = order_mask(count, n) * (1.0 / (5.0 * math.sqrt(2 * n - 1)))
    mask = jnp.concatenate([mask, mask], axis=1)
    pack_ref[me, :n, :] = product(toeplitz, modes) * mask
    order = lax.broadcasted_iota(jnp.int32, (1, n), 1) - n // 2
    window = ((order >= -(count // 2)) & (order < count - count // 2)).astype(F32)
    magnitude = window * jnp.exp(-decay_ref[...])
    phase = phase_ref[...]
    own = jnp.concatenate([magnitude * jnp.cos(phase), magnitude * jnp.sin(phase)], axis=1)
    pack_ref[me, n:, :] = jnp.broadcast_to(own, (8, 2 * n))

    def carry(i, sem, to):
        return pltpu.make_async_remote_copy(
            src_ref=pack_ref.at[i],
            dst_ref=pack_ref.at[i],
            send_sem=sem,
            recv_sem=recv_sem.at[i],
            device_id={"layer": to},
            device_id_type=MESH,
        )

    pl.semaphore_wait(barrier, len(peers))
    sends = [carry(me, send_sem.at[hop], ahead(hop)) for hop in far]
    sends.append(carry(me, send_sem.at[0], other_core))
    for send in sends:
        send.start()
    for hop in far:
        source = behind(hop)
        forward = carry(source, pass_sem.at[hop], other_core)
        forward.wait_recv()
        forward.start()
        sends.append(forward)
    carry(other_core, send_sem.at[0], other_core).wait_recv()
    for hop in far:
        source = lax.rem(other_core + layers - 2 * hop, layers)
        carry(source, pass_sem.at[hop], other_core).wait_recv()

    def sheet(i):
        return pack_ref[i, :n, :]

    def prop(i):
        return pack_ref[i, n : n + 1, :]

    below[...] = scaled(outer(prop(layers - 2)), sheet(layers - 1))

    def go_up(step, carry):
        i = layers - 2 - step
        here = sheet(i)
        start = below[...]
        base = product(split(here), split(start))
        value, _, _ = series(start, base)
        below[...] = scaled(outer(prop(i - 1)), here + both * value)
        return carry

    lax.fori_loop(0, jnp.maximum(layers - 2 - me, 0), go_up, 0)

    @pl.when(me == layers - 1)
    def _():
        below[...] = jnp.zeros_like(below)

    unit = (
        lax.broadcasted_iota(jnp.int32, (n, n), 0) == lax.broadcasted_iota(jnp.int32, (n, n), 1)
    ).astype(F32)
    unit = jnp.concatenate([unit, unit], axis=1)
    back[...] = scaled(outer(prop(0)), sheet(0))
    left[...] = through * unit * prop(0)
    right[...] = through * unit * prop(0)

    def go_down(i, carry):
        here = split(sheet(i))
        value, into, out = back[...], left[...], right[...]
        value_parts = split(value)
        power = product(here, value_parts)
        other = product(value_parts, here)
        for level in range(LEVELS):
            power_parts, other_parts = split(power), split(other)
            weight = weights(power_parts)
            last = level + 1 == LEVELS
            lefts = [split(value), split(into)] + ([] if last else [power_parts])
            steps = products(lefts, weight)
            value, into = value + steps[0], into + steps[1]
            out = out + product(other_parts, split(out))
            if not last:
                power = steps[2]
                other = product(other_parts, other_parts)
        p = prop(i)
        back[...] = scaled(outer(p), sheet(i) + both * value)
        left[...] = through * scaled(into, spread_rows(p))
        right[...] = through * scaled(spread_columns(p), out)
        return carry

    lax.fori_loop(1, jnp.maximum(me, 1), go_down, 0)

    here = sheet(me)
    start = below[...]
    base = product(split(here), split(start))
    value, starts, powers = series(start, base)
    reflection = here + both * value
    bar[...] = conj_transpose(jnp.concatenate([cot_ref[0], cot_ref[1]], axis=1))

    @pl.when(me > 0)
    def _():
        above = split(back[...])
        above_base = product(above, split(reflection))
        _, above_starts, above_powers = series(reflection, above_base)
        inner = product(split(product(split(right[...]), split(bar[...]))), split(left[...]))
        base_bar, start_bar = series_back(above_starts, above_powers, inner, True)
        bar[...] = start_bar + product(split(base_bar), above)

    sheet_bar = bar[...]
    base_bar, _ = series_back(starts, powers, both * sheet_bar, False)
    sheet_bar = sheet_bar + product(split(start), split(base_bar))
    coupled_bar = split(sheet_bar * mask)
    flip = (
        lax.broadcasted_iota(jnp.int32, (n, n), 0) + lax.broadcasted_iota(jnp.int32, (n, n), 1)
        == n - 1
    ).astype(F32).astype(BF16)
    flipped = tuple(real_dot(flip, part).astype(BF16) for part in modes)
    toeplitz_bar = product(flipped, coupled_bar)
    zeros = jnp.zeros((n, n), F32)

    def fold(part):
        wide = jnp.concatenate([part, zeros], axis=1)
        rolled = pltpu.roll(wide, 0, 1, stride=1, stride_axis=0)
        return jnp.sum(rolled, axis=0, keepdims=True)

    eps_slots[wave] = jnp.concatenate(
        [fold(toeplitz_bar[:, :n]), -fold(toeplitz_bar[:, n:]), jnp.zeros((6, 2 * n), F32)], axis=0
    )

    def eps_copy(slot, hop, to):
        return pltpu.make_async_remote_copy(
            src_ref=eps_slots.at[slot],
            dst_ref=eps_slots.at[slot],
            send_sem=eps_send.at[hop],
            recv_sem=eps_recv.at[slot],
            device_id={"wave": to},
            device_id_type=MESH,
        )

    for hop in range(1, waves):
        send = eps_copy(wave, hop, wave_ahead(hop))
        send.start()
        sends.append(send)
    mode_bar = conj_transpose(product(coupled_bar, toeplitz))
    grad_ref[0, 0, 0] = mode_bar[:, :n]
    grad_ref[0, 0, 1] = mode_bar[:, n:]
    for hop in range(1, waves):
        source = lax.rem(wave + waves - hop, waves)
        eps_copy(source, hop, source).wait_recv()
    total = eps_slots[0]
    for slot in range(1, waves):
        total = total + eps_slots[slot]
    eps_ref[0] = total[:2, : 2 * n - 1]
    for send in sends:
        send.wait_send()


def per_device(
    layers,
    waves,
    eps_harmonics,
    eigen_modes,
    mode_phase,
    mode_decay,
    retained_orders,
    reflect_cotangent,
):
    n = eigen_modes.shape[-1]
    vmem = pl.BlockSpec(memory_space=pltpu.VMEM)
    smem = pl.BlockSpec(memory_space=pltpu.SMEM)
    anywhere = pl.BlockSpec(memory_space=pl.ANY)
    dma = pltpu.SemaphoreType.DMA
    wide = pltpu.VMEM((n, 2 * n), F32)
    return pl.pallas_call(
        functools.partial(kernel, layers, waves),
        out_shape=(
            jax.ShapeDtypeStruct(eps_harmonics.shape, F32),
            jax.ShapeDtypeStruct(eigen_modes.shape, F32),
        ),
        in_specs=[smem] + [anywhere] * 5,
        out_specs=(vmem, vmem),
        scratch_shapes=[
            pltpu.VMEM((layers, n + 8, 2 * n), F32),
            pltpu.VMEM((2, 2 * n - 1), F32),
            pltpu.VMEM((2, n, n), F32),
            pltpu.VMEM((1, n), F32),
            pltpu.VMEM((1, n), F32),
            pltpu.VMEM((2, n, n), F32),
            wide,
            wide,
            wide,
            wide,
            wide,
            pltpu.VMEM((waves, 8, 2 * n), F32),
            dma((5,)),
            dma((layers,)),
            dma((layers,)),
            dma((layers,)),
            dma((waves,)),
            dma((waves,)),
        ],
        compiler_params=pltpu.CompilerParams(
            vmem_limit_bytes=48 * 1024 * 1024, collective_id=0, has_side_effects=True
        ),
        name="stack",
    )(retained_orders, eps_harmonics, eigen_modes, mode_phase, mode_decay, reflect_cotangent)


def solution(mesh):
    placed = (
        P("layer", None, None),
        P("layer", "wave", None, None, None),
        P("layer", "wave", None),
        P("layer", "wave", None),
        P("wave"),
        P("wave", None, None, None),
    )
    return jax.shard_map(
        functools.partial(per_device, mesh.shape["layer"], mesh.shape["wave"]),
        mesh=mesh,
        in_specs=placed,
        out_specs=(P("layer", None, None), P("layer", "wave", None, None, None)),
        check_vma=False,
    )
```

```python
import functools
import math

import jax
import jax.numpy as jnp
from jax import lax
from jax.experimental import pallas as pl
from jax.experimental.pallas import tpu as pltpu
from jax.sharding import PartitionSpec as P

TRANSMISSION = 0.9
LEVELS = 5
F32 = jnp.float32
BF16 = jnp.bfloat16
MESH = pl.DeviceIdType.MESH


def split(x):
    hi = x.astype(BF16)
    return hi, (x - hi.astype(F32)).astype(BF16)


def embed(b):
    n = b.shape[0]
    return jnp.concatenate([b, jnp.concatenate([-b[:, n:], b[:, :n]], axis=1)], axis=0)


def weights(parts):
    return embed(parts[0]), embed(parts[1])


def real_dot(a, b):
    return jnp.dot(a, b, preferred_element_type=F32)


def products(lefts, weight):
    n = lefts[0][0].shape[0]
    high, low = weight
    first = real_dot(jnp.concatenate([part for left in lefts for part in left], axis=0), high)
    second = real_dot(jnp.concatenate([left[0] for left in lefts], axis=0), low)
    return [
        first[2 * i * n : (2 * i + 1) * n]
        + first[(2 * i + 1) * n : (2 * i + 2) * n]
        + second[i * n : (i + 1) * n]
        for i in range(len(lefts))
    ]


def product(left, right):
    return products([left], weights(right))[0]


def scaled(a, b):
    n = a.shape[0]
    ar, ai, br, bi = a[:, :n], a[:, n:], b[:, :n], b[:, n:]
    return jnp.concatenate([ar * br - ai * bi, ar * bi + ai * br], axis=1)


def conj_transpose(a):
    n = a.shape[0]
    return jnp.concatenate([a[:, :n].T, -a[:, n:].T], axis=1)


def spread_rows(prop):
    n = prop.shape[-1] // 2
    return jnp.broadcast_to(prop, (n, 2 * n))


def spread_columns(prop):
    n = prop.shape[-1] // 2
    rows = spread_rows(prop)
    return jnp.concatenate([rows[:, :n].T, rows[:, n:].T], axis=1)


def outer(prop):
    return scaled(spread_columns(prop), spread_rows(prop))


def series(start, base):
    starts, powers = [], []
    value, power = start, base
    for level in range(LEVELS):
        value_parts, power_parts = split(value), split(power)
        starts.append(value_parts)
        powers.append(power_parts)
        weight = weights(power_parts)
        if level + 1 < LEVELS:
            step, power = products([value_parts, power_parts], weight)
        else:
            (step,) = products([value_parts], weight)
        value = value + step
    return value, starts, powers


def series_back(starts, powers, cotangent, need_start):
    power_bar = None
    for level in reversed(range(LEVELS)):
        parts = split(cotangent)
        total = product(parts, starts[level])
        if power_bar is not None:
            bar_parts = split(power_bar)
            total = total + product(bar_parts, powers[level])
            total = total + product(powers[level], bar_parts)
        if level > 0 or need_start:
            cotangent = cotangent + product(powers[level], parts)
        power_bar = total
    return power_bar, cotangent


def order_mask(count, n):
    half = count // 2
    row = lax.broadcasted_iota(jnp.int32, (n, n), 0) - n // 2
    column = lax.broadcasted_iota(jnp.int32, (n, n), 1) - n // 2
    keep = (row >= -half) & (row < count - half) & (column >= -half) & (column < count - half)
    return keep.astype(F32)


def toeplitz_of(harm_ref, n):
    def one(part):
        harmonics = jnp.concatenate([harm_ref[part : part + 1, :], jnp.zeros((1, 1), F32)], axis=1)
        rows = jnp.broadcast_to(harmonics, (n, 2 * n))
        rolled = pltpu.roll(rows, n + 1, 1, stride=1, stride_axis=0)
        return rolled[:, :n].T

    return jnp.concatenate([one(0), one(1)], axis=1)


def kernel(
    layers, waves, count_ref, harm_in, mode_in, phase_in, decay_in, cot_in, eps_ref, grad_ref,
    pack_ref, harm_ref, mode_ref, phase_ref, decay_ref, cot_ref, below, back, left, right, bar,
    eps_slots, in_sem, send_sem, recv_sem, pass_sem, eps_send, eps_recv,
):
    n = mode_ref.shape[-1]
    through = TRANSMISSION
    both = through * through
    me = lax.axis_index("layer")
    wave = lax.axis_index("wave")
    other_core = me + 1 - 2 * lax.rem(me, 2)
    far = range(1, layers // 2)

    def ahead(hop):
        return lax.rem(me + 2 * hop, layers)

    def wave_ahead(hop):
        return lax.rem(wave + hop, waves)

    loads = [
        pltpu.make_async_copy(source, target, in_sem.at[i])
        for i, (source, target) in enumerate(
            (
                (harm_in.at[0], harm_ref),
                (mode_in.at[0, 0], mode_ref),
                (phase_in.at[0], phase_ref),
                (decay_in.at[0], decay_ref),
                (cot_in.at[0], cot_ref),
            )
        )
    ]
    for load in loads:
        load.start()
    barrier = pltpu.get_barrier_semaphore()
    peers = [{"layer": other_core}] + [{"layer": ahead(hop)} for hop in far]
    peers = peers + [{"wave": wave_ahead(hop)} for hop in range(1, waves)]
    for peer in peers:
        pl.semaphore_signal(barrier, inc=1, device_id=peer, device_id_type=MESH)
    for load in loads[:4]:
        load.wait()

    count = count_ref[0]
    modes = split(jnp.concatenate([mode_ref[0], mode_ref[1]], axis=1))
    toeplitz = split(toeplitz_of(harm_ref, n))
    mask = order_mask(count, n) * (1.0 / (5.0 * math.sqrt(2 * n - 1)))
    mask = jnp.concatenate([mask, mask], axis=1)
    pack_ref[me, :n, :] = product(toeplitz, modes) * mask
    order = lax.broadcasted_iota(jnp.int32, (1, n), 1) - n // 2
    window = ((order >= -(count // 2)) & (order < count - count // 2)).astype(F32)
    magnitude = window * jnp.exp(-decay_ref[...])
    phase = phase_ref[...]
    own = jnp.concatenate([magnitude * jnp.cos(phase), magnitude * jnp.sin(phase)], axis=1)
    pack_ref[me, n:, :] = jnp.broadcast_to(own, (8, 2 * n))

    def carry(i, sem, to):
        return pltpu.make_async_remote_copy(
            src_ref=pack_ref.at[i],
            dst_ref=pack_ref.at[i],
            send_sem=sem,
            recv_sem=recv_sem.at[i],
            device_id={"layer": to},
            device_id_type=MESH,
        )

    pl.semaphore_wait(barrier, len(peers))
    sends = [carry(me, send_sem.at[0], other_core)]
    sends = sends + [carry(me, send_sem.at[hop], ahead(hop)) for hop in far]
    for send in sends:
        send.start()
    carry(other_core, send_sem.at[0], other_core).wait_recv()
    core = lax.rem(me, 2)
    pair = me // 2
    pairs = layers // 2

    def receive(q):
        near = 2 * q + core
        forward = carry(near, pass_sem.at[q], other_core)
        forward.wait_recv()
        forward.start()
        across = 2 * q + 1 - core
        carry(across, pass_sem.at[q], other_core).wait_recv()

    def sheet(i):
        return pack_ref[i, :n, :]

    def prop(i):
        return pack_ref[i, n : n + 1, :]

    def go_up(i, token):
        here = sheet(i)
        start = scaled(outer(prop(i)), below[...])
        base = product(split(here), split(start))
        value, _, _ = series(start, base)
        below[...] = here + both * value
        return token

    def pair_up(step, token):
        q = pairs - 1 - step
        receive(q)

        @pl.when(step == 0)
        def _():
            below[...] = sheet(layers - 1)

        first = jnp.where(step == 0, 1, 0)
        lax.fori_loop(first, 2, lambda k, t: go_up(2 * q + 1 - k, t), 0)
        return token

    lax.fori_loop(0, pairs - 1 - pair, pair_up, 0)

    @pl.when(pair == pairs - 1)
    def _():
        below[...] = sheet(layers - 1)

    @pl.when((core == 0) & (pair < pairs - 1))
    def _():
        go_up(me + 1, 0)

    def first_layer():
        unit = (
            lax.broadcasted_iota(jnp.int32, (n, n), 0)
            == lax.broadcasted_iota(jnp.int32, (n, n), 1)
        ).astype(F32)
        unit = jnp.concatenate([unit, unit], axis=1)
        back[...] = scaled(outer(prop(0)), sheet(0))
        left[...] = through * unit * prop(0)
        right[...] = through * unit * prop(0)

    def go_down(i, token):
        here = split(sheet(i))
        value, into, out = back[...], left[...], right[...]
        value_parts = split(value)
        power = product(here, value_parts)
        other = product(value_parts, here)
        for level in range(LEVELS):
            power_parts, other_parts = split(power), split(other)
            weight = weights(power_parts)
            last = level + 1 == LEVELS
            lefts = [split(value), split(into)] + ([] if last else [power_parts])
            steps = products(lefts, weight)
            value, into = value + steps[0], into + steps[1]
            out = out + product(other_parts, split(out))
            if not last:
                power = steps[2]
                other = product(other_parts, other_parts)
        p = prop(i)
        back[...] = scaled(outer(p), sheet(i) + both * value)
        left[...] = through * scaled(into, spread_rows(p))
        right[...] = through * scaled(spread_columns(p), out)
        return token

    def pair_down(q, token):
        receive(q)

        @pl.when(q == 0)
        def _():
            first_layer()

        first = jnp.where(q == 0, 1, 0)
        lax.fori_loop(2 * q + first, 2 * q + 2, go_down, 0)
        return token

    lax.fori_loop(0, pair, pair_down, 0)

    @pl.when(me == 1)
    def _():
        first_layer()

    @pl.when((core == 1) & (pair > 0))
    def _():
        go_down(me - 1, 0)

    loads[4].wait()

    def own_layer(has_below):
        reflection = here = sheet(me)
        if has_below:
            start = scaled(outer(prop(me)), below[...])
            base = product(split(here), split(start))
            value, starts, powers = series(start, base)
            reflection = here + both * value
        bar[...] = conj_transpose(jnp.concatenate([cot_ref[0], cot_ref[1]], axis=1))

        @pl.when(me > 0)
        def _():
            above = split(back[...])
            above_base = product(above, split(reflection))
            _, above_starts, above_powers = series(reflection, above_base)
            inner = product(split(product(split(right[...]), split(bar[...]))), split(left[...]))
            base_bar, start_bar = series_back(above_starts, above_powers, inner, True)
            bar[...] = start_bar + product(split(base_bar), above)

        if has_below:
            base_bar, _ = series_back(starts, powers, both * bar[...], False)
            bar[...] += product(split(start), split(base_bar))

    @pl.when(me < layers - 1)
    def _():
        own_layer(True)

    @pl.when(me == layers - 1)
    def _():
        own_layer(False)

    sheet_bar = bar[...]
    coupled_bar = split(sheet_bar * mask)
    flip = (
        lax.broadcasted_iota(jnp.int32, (n, n), 0) + lax.broadcasted_iota(jnp.int32, (n, n), 1)
        == n - 1
    ).astype(F32).astype(BF16)
    flipped = tuple(real_dot(flip, part).astype(BF16) for part in modes)
    toeplitz_bar = product(flipped, coupled_bar)
    zeros = jnp.zeros((n, n), F32)

    def fold(part):
        wide = jnp.concatenate([part, zeros], axis=1)
        rolled = pltpu.roll(wide, 0, 1, stride=1, stride_axis=0)
        return jnp.sum(rolled, axis=0, keepdims=True)

    eps_slots[wave] = jnp.concatenate(
        [fold(toeplitz_bar[:, :n]), -fold(toeplitz_bar[:, n:]), jnp.zeros((6, 2 * n), F32)], axis=0
    )

    def eps_copy(slot, hop, to):
        return pltpu.make_async_remote_copy(
            src_ref=eps_slots.at[slot],
            dst_ref=eps_slots.at[slot],
            send_sem=eps_send.at[hop],
            recv_sem=eps_recv.at[slot],
            device_id={"wave": to},
            device_id_type=MESH,
        )

    for hop in range(1, waves):
        send = eps_copy(wave, hop, wave_ahead(hop))
        send.start()
        sends.append(send)
    mode_bar = conj_transpose(product(coupled_bar, toeplitz))
    grad_ref[0, 0, 0] = mode_bar[:, :n]
    grad_ref[0, 0, 1] = mode_bar[:, n:]
    for hop in range(1, waves):
        source = lax.rem(wave + waves - hop, waves)
        eps_copy(source, hop, source).wait_recv()
    total = eps_slots[0]
    for slot in range(1, waves):
        total = total + eps_slots[slot]
    eps_ref[0] = total[:2, : 2 * n - 1]
    for send in sends:
        send.wait_send()
    for hop in far:
        q = lax.rem(pair + hop, pairs)
        carry(2 * q + core, pass_sem.at[q], other_core).wait_send()


def per_device(
    layers,
    waves,
    eps_harmonics,
    eigen_modes,
    mode_phase,
    mode_decay,
    retained_orders,
    reflect_cotangent,
):
    n = eigen_modes.shape[-1]
    vmem = pl.BlockSpec(memory_space=pltpu.VMEM)
    smem = pl.BlockSpec(memory_space=pltpu.SMEM)
    hbm = pl.BlockSpec(memory_space=pltpu.HBM)
    dma = pltpu.SemaphoreType.DMA
    wide = pltpu.VMEM((n, 2 * n), F32)
    return pl.pallas_call(
        functools.partial(kernel, layers, waves),
        out_shape=(
            jax.ShapeDtypeStruct(eps_harmonics.shape, F32),
            jax.ShapeDtypeStruct(eigen_modes.shape, F32),
        ),
        in_specs=[smem] + [hbm] * 5,
        out_specs=(vmem, vmem),
        scratch_shapes=[
            pltpu.VMEM((layers, n + 8, 2 * n), F32),
            pltpu.VMEM((2, 2 * n - 1), F32),
            pltpu.VMEM((2, n, n), F32),
            pltpu.VMEM((1, n), F32),
            pltpu.VMEM((1, n), F32),
            pltpu.VMEM((2, n, n), F32),
            wide,
            wide,
            wide,
            wide,
            wide,
            pltpu.VMEM((waves, 8, 2 * n), F32),
            dma((5,)),
            dma((layers,)),
            dma((layers,)),
            dma((layers,)),
            dma((waves,)),
            dma((waves,)),
        ],
        compiler_params=pltpu.CompilerParams(
            vmem_limit_bytes=48 * 1024 * 1024, collective_id=0, has_side_effects=True
        ),
        name="stack",
    )(retained_orders, eps_harmonics, eigen_modes, mode_phase, mode_decay, reflect_cotangent)


def solution(mesh):
    placed = (
        P("layer", None, None),
        P("layer", "wave", None, None, None),
        P("layer", "wave", None),
        P("layer", "wave", None),
        P("wave"),
        P("wave", None, None, None),
    )
    return jax.shard_map(
        functools.partial(per_device, mesh.shape["layer"], mesh.shape["wave"]),
        mesh=mesh,
        in_specs=placed,
        out_specs=(P("layer", None, None), P("layer", "wave", None, None, None)),
        check_vma=False,
    )
```

```python
import functools
import math

import jax
import jax.numpy as jnp
from jax import lax
from jax.experimental import pallas as pl
from jax.experimental.pallas import tpu as pltpu
from jax.sharding import PartitionSpec as P

TRANSMISSION = 0.9
LEVELS = 5
F32 = jnp.float32
BF16 = jnp.bfloat16
MESH = pl.DeviceIdType.MESH


def split(x):
    hi = x.astype(BF16)
    return hi, (x - hi.astype(F32)).astype(BF16)


def embed(b):
    n = b.shape[0]
    return jnp.concatenate([b, jnp.concatenate([-b[:, n:], b[:, :n]], axis=1)], axis=0)


def weights(parts):
    return embed(parts[0]), embed(parts[1])


def real_dot(a, b):
    return jnp.dot(a, b, preferred_element_type=F32)


def products(lefts, weight):
    n = lefts[0][0].shape[0]
    high, low = weight
    first = real_dot(jnp.concatenate([part for left in lefts for part in left], axis=0), high)
    second = real_dot(jnp.concatenate([left[0] for left in lefts], axis=0), low)
    return [
        first[2 * i * n : (2 * i + 1) * n]
        + first[(2 * i + 1) * n : (2 * i + 2) * n]
        + second[i * n : (i + 1) * n]
        for i in range(len(lefts))
    ]


def products_of_one(left, weight):
    return products([left], weight)[0]


def product(left, right):
    return products_of_one(left, weights(right))


def single(left, weight):
    return real_dot(left[0], weight[0])


def scaled(a, b):
    n = a.shape[0]
    ar, ai, br, bi = a[:, :n], a[:, n:], b[:, :n], b[:, n:]
    return jnp.concatenate([ar * br - ai * bi, ar * bi + ai * br], axis=1)


def conj_transpose(a):
    n = a.shape[0]
    return jnp.concatenate([a[:, :n].T, -a[:, n:].T], axis=1)


def spread_rows(prop):
    n = prop.shape[-1] // 2
    return jnp.broadcast_to(prop, (n, 2 * n))


def spread_columns(prop):
    n = prop.shape[-1] // 2
    rows = spread_rows(prop)
    return jnp.concatenate([rows[:, :n].T, rows[:, n:].T], axis=1)


def outer(prop):
    return scaled(spread_columns(prop), spread_rows(prop))


def series(start, base):
    starts, powers = [], []
    value, power = start, base
    for level in range(LEVELS):
        value_parts, power_parts = split(value), split(power)
        starts.append(value_parts)
        powers.append(power_parts)
        weight = weights(power_parts)
        if level + 2 < LEVELS:
            step, power = products([value_parts, power_parts], weight)
        elif level + 1 < LEVELS:
            (step,) = products([value_parts], weight)
            power = single(power_parts, weight)
        else:
            step = single(value_parts, weight)
        value = value + step
    return value, starts, powers


def series_back(starts, powers, cotangent, need_start):
    power_bar = None
    for level in reversed(range(LEVELS)):
        parts = split(cotangent)
        total = product(parts, starts[level])
        if power_bar is not None:
            bar_parts = split(power_bar)
            total = total + product(bar_parts, powers[level])
            total = total + product(powers[level], bar_parts)
        if level > 0 or need_start:
            form = single if level + 1 == LEVELS else products_of_one
            cotangent = cotangent + form(powers[level], weights(parts))
        power_bar = total
    return power_bar, cotangent


def order_mask(count, n):
    half = count // 2
    row = lax.broadcasted_iota(jnp.int32, (n, n), 0) - n // 2
    column = lax.broadcasted_iota(jnp.int32, (n, n), 1) - n // 2
    keep = (row >= -half) & (row < count - half) & (column >= -half) & (column < count - half)
    return keep.astype(F32)


def toeplitz_of(harm_ref, n):
    def one(part):
        harmonics = jnp.concatenate([harm_ref[part : part + 1, :], jnp.zeros((1, 1), F32)], axis=1)
        rows = jnp.broadcast_to(harmonics, (n, 2 * n))
        rolled = pltpu.roll(rows, n + 1, 1, stride=1, stride_axis=0)
        return rolled[:, :n].T

    return jnp.concatenate([one(0), one(1)], axis=1)


def kernel(
    layers, waves, count_ref, harm_in, mode_in, phase_in, decay_in, cot_in, eps_ref, grad_ref,
    pack_ref, harm_ref, mode_ref, phase_ref, decay_ref, cot_ref, below, back, left, right, bar,
    eps_slots, in_sem, send_sem, recv_sem, pass_sem, eps_send, eps_recv,
):
    n = mode_ref.shape[-1]
    through = TRANSMISSION
    both = through * through
    me = lax.axis_index("layer")
    wave = lax.axis_index("wave")
    other_core = me + 1 - 2 * lax.rem(me, 2)
    far = range(1, layers // 2)

    def ahead(hop):
        return lax.rem(me + 2 * hop, layers)

    def wave_ahead(hop):
        return lax.rem(wave + hop, waves)

    loads = [
        pltpu.make_async_copy(source, target, in_sem.at[i])
        for i, (source, target) in enumerate(
            (
                (harm_in.at[0], harm_ref),
                (mode_in.at[0, 0], mode_ref),
                (phase_in.at[0], phase_ref),
                (decay_in.at[0], decay_ref),
                (cot_in.at[0], cot_ref),
            )
        )
    ]
    for load in loads:
        load.start()
    barrier = pltpu.get_barrier_semaphore()
    peers = [{"layer": other_core}] + [{"layer": ahead(hop)} for hop in far]
    peers = peers + [{"wave": wave_ahead(hop)} for hop in range(1, waves)]
    for peer in peers:
        pl.semaphore_signal(barrier, inc=1, device_id=peer, device_id_type=MESH)
    for load in loads[:4]:
        load.wait()

    count = count_ref[0]
    modes = split(jnp.concatenate([mode_ref[0], mode_ref[1]], axis=1))
    toeplitz = split(toeplitz_of(harm_ref, n))
    mask = order_mask(count, n) * (1.0 / (5.0 * math.sqrt(2 * n - 1)))
    mask = jnp.concatenate([mask, mask], axis=1)
    pack_ref[me, :n, :] = product(toeplitz, modes) * mask
    order = lax.broadcasted_iota(jnp.int32, (1, n), 1) - n // 2
    window = ((order >= -(count // 2)) & (order < count - count // 2)).astype(F32)
    magnitude = window * jnp.exp(-decay_ref[...])
    phase = phase_ref[...]
    own = jnp.concatenate([magnitude * jnp.cos(phase), magnitude * jnp.sin(phase)], axis=1)
    pack_ref[me, n:, :] = jnp.broadcast_to(own, (8, 2 * n))

    def carry(i, sem, to):
        return pltpu.make_async_remote_copy(
            src_ref=pack_ref.at[i],
            dst_ref=pack_ref.at[i],
            send_sem=sem,
            recv_sem=recv_sem.at[i],
            device_id={"layer": to},
            device_id_type=MESH,
        )

    pl.semaphore_wait(barrier, len(peers))
    sends = [carry(me, send_sem.at[0], other_core)]
    sends = sends + [carry(me, send_sem.at[hop], ahead(hop)) for hop in far]
    for send in sends:
        send.start()
    carry(other_core, send_sem.at[0], other_core).wait_recv()
    core = lax.rem(me, 2)
    pair = me // 2
    pairs = layers // 2

    def receive(q):
        near = 2 * q + core
        forward = carry(near, pass_sem.at[q], other_core)
        forward.wait_recv()
        forward.start()
        across = 2 * q + 1 - core
        carry(across, pass_sem.at[q], other_core).wait_recv()

    def sheet(i):
        return pack_ref[i, :n, :]

    def prop(i):
        return pack_ref[i, n : n + 1, :]

    def go_up(i, token):
        here = sheet(i)
        start = scaled(outer(prop(i)), below[...])
        base = product(split(here), split(start))
        value, _, _ = series(start, base)
        below[...] = here + both * value
        return token

    def pair_up(step, token):
        q = pairs - 1 - step
        receive(q)

        @pl.when(step == 0)
        def _():
            below[...] = sheet(layers - 1)

        first = jnp.where(step == 0, 1, 0)
        lax.fori_loop(first, 2, lambda k, t: go_up(2 * q + 1 - k, t), 0)
        return token

    lax.fori_loop(0, pairs - 1 - pair, pair_up, 0)

    @pl.when(pair == pairs - 1)
    def _():
        below[...] = sheet(layers - 1)

    @pl.when((core == 0) & (pair < pairs - 1))
    def _():
        go_up(me + 1, 0)

    def first_layer():
        unit = (
            lax.broadcasted_iota(jnp.int32, (n, n), 0)
            == lax.broadcasted_iota(jnp.int32, (n, n), 1)
        ).astype(F32)
        unit = jnp.concatenate([unit, unit], axis=1)
        back[...] = scaled(outer(prop(0)), sheet(0))
        left[...] = through * unit * prop(0)
        right[...] = through * unit * prop(0)

    def go_down(i, token):
        here = split(sheet(i))
        value, into, out = back[...], left[...], right[...]
        value_parts = split(value)
        power = product(here, value_parts)
        other = product(value_parts, here)
        for level in range(LEVELS):
            power_parts, other_parts = split(power), split(other)
            weight = weights(power_parts)
            out_weight = weights(split(out))
            if level + 1 == LEVELS:
                value = value + single(split(value), weight)
                into = into + single(split(into), weight)
                out = out + single(other_parts, out_weight)
                break
            out = out + products_of_one(other_parts, out_weight)
            lefts = [split(value), split(into)]
            if level + 2 == LEVELS:
                steps = products(lefts, weight)
                power = single(power_parts, weight)
                other = single(other_parts, weights(other_parts))
            else:
                steps = products(lefts + [power_parts], weight)
                power = steps[2]
                other = product(other_parts, other_parts)
            value, into = value + steps[0], into + steps[1]
        p = prop(i)
        back[...] = scaled(outer(p), sheet(i) + both * value)
        left[...] = through * scaled(into, spread_rows(p))
        right[...] = through * scaled(spread_columns(p), out)
        return token

    def pair_down(q, token):
        receive(q)

        @pl.when(q == 0)
        def _():
            first_layer()

        first = jnp.where(q == 0, 1, 0)
        lax.fori_loop(2 * q + first, 2 * q + 2, go_down, 0)
        return token

    lax.fori_loop(0, pair, pair_down, 0)

    @pl.when(me == 1)
    def _():
        first_layer()

    @pl.when((core == 1) & (pair > 0))
    def _():
        go_down(me - 1, 0)

    loads[4].wait()

    def own_layer(has_below):
        reflection = here = sheet(me)
        if has_below:
            start = scaled(outer(prop(me)), below[...])
            base = product(split(here), split(start))
            value, starts, powers = series(start, base)
            reflection = here + both * value
        bar[...] = conj_transpose(jnp.concatenate([cot_ref[0], cot_ref[1]], axis=1))

        @pl.when(me > 0)
        def _():
            above = split(back[...])
            above_base = product(above, split(reflection))
            _, above_starts, above_powers = series(reflection, above_base)
            inner = product(split(product(split(right[...]), split(bar[...]))), split(left[...]))
            base_bar, start_bar = series_back(above_starts, above_powers, inner, True)
            bar[...] = start_bar + product(split(base_bar), above)

        if has_below:
            base_bar, _ = series_back(starts, powers, both * bar[...], False)
            bar[...] += product(split(start), split(base_bar))

    @pl.when(me < layers - 1)
    def _():
        own_layer(True)

    @pl.when(me == layers - 1)
    def _():
        own_layer(False)

    sheet_bar = bar[...]
    coupled_bar = split(sheet_bar * mask)
    flip = (
        lax.broadcasted_iota(jnp.int32, (n, n), 0) + lax.broadcasted_iota(jnp.int32, (n, n), 1)
        == n - 1
    ).astype(F32).astype(BF16)
    flipped = tuple(real_dot(flip, part).astype(BF16) for part in modes)
    toeplitz_bar = product(flipped, coupled_bar)
    zeros = jnp.zeros((n, n), F32)

    def fold(part):
        wide = jnp.concatenate([part, zeros], axis=1)
        rolled = pltpu.roll(wide, 0, 1, stride=1, stride_axis=0)
        return jnp.sum(rolled, axis=0, keepdims=True)

    eps_slots[wave] = jnp.concatenate(
        [fold(toeplitz_bar[:, :n]), -fold(toeplitz_bar[:, n:]), jnp.zeros((6, 2 * n), F32)], axis=0
    )

    def eps_copy(slot, hop, to):
        return pltpu.make_async_remote_copy(
            src_ref=eps_slots.at[slot],
            dst_ref=eps_slots.at[slot],
            send_sem=eps_send.at[hop],
            recv_sem=eps_recv.at[slot],
            device_id={"wave": to},
            device_id_type=MESH,
        )

    for hop in range(1, waves):
        send = eps_copy(wave, hop, wave_ahead(hop))
        send.start()
        sends.append(send)
    mode_bar = conj_transpose(product(coupled_bar, toeplitz))
    grad_ref[0, 0, 0] = mode_bar[:, :n]
    grad_ref[0, 0, 1] = mode_bar[:, n:]
    for hop in range(1, waves):
        source = lax.rem(wave + waves - hop, waves)
        eps_copy(source, hop, source).wait_recv()
    total = eps_slots[0]
    for slot in range(1, waves):
        total = total + eps_slots[slot]
    eps_ref[0] = total[:2, : 2 * n - 1]
    for send in sends:
        send.wait_send()
    for hop in far:
        q = lax.rem(pair + hop, pairs)
        carry(2 * q + core, pass_sem.at[q], other_core).wait_send()


def per_device(
    layers,
    waves,
    eps_harmonics,
    eigen_modes,
    mode_phase,
    mode_decay,
    retained_orders,
    reflect_cotangent,
):
    n = eigen_modes.shape[-1]
    vmem = pl.BlockSpec(memory_space=pltpu.VMEM)
    smem = pl.BlockSpec(memory_space=pltpu.SMEM)
    hbm = pl.BlockSpec(memory_space=pltpu.HBM)
    dma = pltpu.SemaphoreType.DMA
    wide = pltpu.VMEM((n, 2 * n), F32)
    return pl.pallas_call(
        functools.partial(kernel, layers, waves),
        out_shape=(
            jax.ShapeDtypeStruct(eps_harmonics.shape, F32),
            jax.ShapeDtypeStruct(eigen_modes.shape, F32),
        ),
        in_specs=[smem] + [hbm] * 5,
        out_specs=(vmem, vmem),
        scratch_shapes=[
            pltpu.VMEM((layers, n + 8, 2 * n), F32),
            pltpu.VMEM((2, 2 * n - 1), F32),
            pltpu.VMEM((2, n, n), F32),
            pltpu.VMEM((1, n), F32),
            pltpu.VMEM((1, n), F32),
            pltpu.VMEM((2, n, n), F32),
            wide,
            wide,
            wide,
            wide,
            wide,
            pltpu.VMEM((waves, 8, 2 * n), F32),
            dma((5,)),
            dma((layers,)),
            dma((layers,)),
            dma((layers,)),
            dma((waves,)),
            dma((waves,)),
        ],
        compiler_params=pltpu.CompilerParams(
            vmem_limit_bytes=48 * 1024 * 1024, collective_id=0, has_side_effects=True
        ),
        name="stack",
    )(retained_orders, eps_harmonics, eigen_modes, mode_phase, mode_decay, reflect_cotangent)


def solution(mesh):
    placed = (
        P("layer", None, None),
        P("layer", "wave", None, None, None),
        P("layer", "wave", None),
        P("layer", "wave", None),
        P("wave"),
        P("wave", None, None, None),
    )
    return jax.shard_map(
        functools.partial(per_device, mesh.shape["layer"], mesh.shape["wave"]),
        mesh=mesh,
        in_specs=placed,
        out_specs=(P("layer", None, None), P("layer", "wave", None, None, None)),
        check_vma=False,
    )
```
